32 devices in a mesh: groups: 2 (over y), gx: 4 (over x, core), gy: 4 (over z).
Axes of the slice: x: 2, y: 2, z: 4, core: 2. Of those that a mesh axis runs over, the one named last changes fastest.
Arguments:
- activations: bfloat16 [512, 8192], P('groups', ('gx', 'gy')), parts along dimension 0, may hold values from -6 to 6
- gate_up: bfloat16 [8192, 2, 26624], P('gx', None, 'gy'), may hold values from -0.0625 to 0.0625
Outputs:
- hidden: bfloat16 [512, 26624], P(('groups', 'gx'), 'gy'), parts along dimension 0
The draws below stay inside these ranges and needn't reach their ends.
There are 2 independent parts, one for each index of `groups`. The reference program is written for one: setup_inputs(seed, part) draws one part's arguments, and reference() takes and returns one part's arrays. A program takes and returns all parts, laid end to end along the dimension named above; an argument that names none is the same for every part. Nothing has to cross between parts.
All inputs are finite; a program needn't handle non-finite values.
Results may differ from the reference program's by a relative error of at most 0.015.
Values may be sent and summed in bfloat16 or wider, within the bound.
A program may use at most 128 MiB of HBM per device.

```python
import jax
import jax.numpy as jnp
from jax import lax

D = 8192
FF = 26624
ROWS = 256
N_GX = 4


def shard_levels(stream_key, dims, shards, least, high):
    def one(position, blocks):
        steps = jax.random.uniform(jax.random.fold_in(jax.random.fold_in(stream_key, 6), position), (blocks,), jnp.float32, least / len(shards), high / len(shards))
        return jnp.repeat(jnp.exp(steps), dims[position] // blocks).reshape((-1,) + (1,) * (len(dims) - position - 1))

    gain = one(*shards[0])
    for cut in shards[1:]:
        gain = gain * one(*cut)
    return gain


def gaussian(key, dims, deviation, most, cuts=(), held_as=jnp.bfloat16):
    array = jax.random.normal(key, dims, jnp.float32) * deviation
    if len(cuts) > 0:
        array = shard_levels(key, dims, cuts, -0.22, 0.18) * array
    return jnp.clip(array, min=-most, max=most).astype(held_as)


def setup_inputs(seed: int = 0, part: int = 0) -> dict:
    splits = jax.random.split(jax.random.key(seed), 3)
    own_keys = jax.random.split(jax.random.fold_in(splits[2], part), 3)
    activations = gaussian(own_keys[0], (ROWS, D), 1.0, 6.0, ((1, 16),))
    gate_up = gaussian(splits[1], (D, 2, FF), D ** -0.5, 0.0625, ((0, 4), (2, 4)))
    return dict(activations=activations, gate_up=gate_up)


def reference(activations, gate_up):
    block = D // N_GX
    pieces = activations.reshape(ROWS, N_GX, block).transpose(1, 0, 2)
    blocks = gate_up.reshape(N_GX, block, 2, FF)

    def accumulate(total, pair):
        piece, weights = pair
        term = jnp.einsum("rd,dkf->rkf", piece.astype(jnp.float32), weights.astype(jnp.float32))
        rounded = lax.optimization_barrier(term.astype(jnp.bfloat16))
        return total + rounded.astype(jnp.float32), None

    start = jnp.zeros((ROWS, 2, FF), jnp.float32)
    projected, unused = lax.scan(accumulate, start, (pieces, blocks))
    hidden = jax.nn.silu(projected[:, 0]) * projected[:, 1]
    return hidden.astype(jnp.bfloat16)
```

```python
import jax
import jax.numpy as jnp
from jax import lax
from jax.experimental import pallas as pl
from jax.experimental.pallas import tpu as pltpu
from jax.sharding import PartitionSpec as P

MESH = pl.DeviceIdType.MESH
TILE = 256
HALF = 128
RESIDENT = 14
STREAM = 4


def kernel(
    a, w, out, a_all, a2, wbuf, s1, r1, keep, s2, r2,
    wsem, ag_s, ag_r, s1_s, s1_r, s2_s, s2_r,
):
    nz = a_all.shape[0] + 1
    width = a.shape[1]
    block = a.shape[0] // 4
    depth = nz * width
    nt = s2.shape[0]
    resident, stream = min(RESIDENT, nt), STREAM
    cycle = nt - resident
    z, gx = lax.axis_index("gy"), lax.axis_index("gx")
    x, c = gx // 2, gx % 2
    core_peer = 2 * x + 1 - c
    chip_peer = 2 * (1 - x) + c

    def w_copies(tile, slot):
        return [
            pltpu.make_async_copy(w.at[:, 2 * tile + h], wbuf.at[slot, h], wsem.at[slot, h])
            for h in range(2)
        ]

    def load(tile, slot):
        for copy in w_copies(tile, slot):
            copy.start()

    def load_stream(m):
        load(resident + m % cycle, resident + m % stream)

    barrier = pltpu.get_barrier_semaphore()
    for i in range(1, nz):
        pl.semaphore_signal(barrier, inc=1, device_id={"gy": (z + i) % nz}, device_id_type=MESH)
    for peer in (core_peer, chip_peer):
        pl.semaphore_signal(barrier, inc=1, device_id={"gx": peer}, device_id_type=MESH)

    def load_first(t, carry):
        load(t, t)
        return carry

    lax.fori_loop(0, 2, load_first, 0)
    pl.semaphore_wait(barrier, nz + 1)

    def gather(i, phase):
        side = 1 - x if phase == 0 else x
        rows = pl.ds(pl.multiple_of(side * 2 * block, 2 * block), 2 * block)
        return pltpu.make_async_remote_copy(
            src_ref=a.at[rows],
            dst_ref=a_all.at[i - 1, rows],
            send_sem=ag_s.at[i - 1, phase],
            recv_sem=ag_r.at[i - 1, phase],
            device_id={"gy": (z + i) % nz},
            device_id_type=MESH,
        )

    for phase in range(2):
        for i in range(1, nz):
            gather(i, phase).start()
    lax.fori_loop(2, resident, load_first, 0)
    if cycle:
        for m in range(min(stream, 2 * cycle)):
            load_stream(m)

    feature = lax.broadcasted_iota(jnp.int32, (HALF, 4 * HALF), 0)
    place = lax.broadcasted_iota(jnp.int32, (HALF, 4 * HALF), 1)
    spread = (place == 2 * feature + jnp.where(place < 2 * HALF, 0, 2 * HALF + 1)).astype(jnp.bfloat16)

    def widen(phase):
        side = 1 - x if phase == 0 else x
        for i in range(nz):
            source = (z + nz - i) % nz
            if i:
                gather(i, phase).wait_recv()
            for q in range(2):
                core = c if q == 0 else 1 - c
                rows = pl.ds(pl.multiple_of((2 * side + core) * block, block), block)
                for j in range(width // HALF):
                    lanes = pl.ds(j * HALF, HALF)
                    piece = a[rows, lanes] if i == 0 else a_all[i - 1, rows, lanes]
                    both = jnp.dot(piece, spread, preferred_element_type=jnp.float32).astype(jnp.bfloat16)
                    to = pl.ds(pl.multiple_of(source * 2 * width + j * 2 * HALF, 2 * HALF), 2 * HALF)
                    a2[phase, pl.ds(q * 2 * block, block), to] = both[:, : 2 * HALF]
                    a2[phase, pl.ds(q * 2 * block + block, block), to] = both[:, 2 * HALF :]

    def to_core(i):
        return pltpu.make_async_remote_copy(
            src_ref=s1.at[i], dst_ref=r1.at[i], send_sem=s1_s.at[i], recv_sem=s1_r.at[i],
            device_id={"gx": core_peer}, device_id_type=MESH,
        )

    def to_chip(t):
        return pltpu.make_async_remote_copy(
            src_ref=s2.at[t], dst_ref=r2.at[t], send_sem=s2_s.at[t], recv_sem=s2_r.at[t],
            device_id={"gx": chip_peer}, device_id_type=MESH,
        )

    def chip_sum(i):
        to_core(i).wait_recv()
        return keep[i % 2] + r1[i].astype(jnp.float32)

    def pass_on(t):
        s2[t] = chip_sum(t).astype(jnp.bfloat16)
        to_chip(t).start()

    def finish(t):
        total = chip_sum(nt + t)
        to_chip(t).wait_recv()
        total = total + r2[t].astype(jnp.float32)
        gate, up = total[:block], total[block:]
        hidden = gate / (1.0 + jnp.exp(-gate)) * up
        out[:, pl.ds(pl.multiple_of(t * TILE, TILE), TILE)] = hidden.astype(jnp.bfloat16)

    def step(i, carry):
        phase = i // nt
        t = i % nt
        m = phase * cycle + t - resident
        held = t < resident
        slot = jnp.where(held, t, resident + (m + stream) % stream)

        @pl.when(jnp.logical_or(phase == 0, jnp.logical_not(held)))
        def arrive():
            for copy in w_copies(t, slot):
                copy.wait()

        weights = jnp.concatenate(
            [wbuf.at[slot, h].reshape(2 * depth, HALF)[...] for h in range(2)], axis=1
        )
        value = jnp.dot(a2[phase], weights, preferred_element_type=jnp.float32)
        s1[i] = value[2 * block :].astype(jnp.bfloat16)
        to_core(i).start()
        keep[i % 2] = value[: 2 * block]

        if cycle:
            @pl.when(jnp.logical_and(jnp.logical_not(held), m + stream < 2 * cycle))
            def refill():
                load_stream(m + stream)

        @pl.when(jnp.logical_and(i >= 1, i <= nt))
        def send():
            pass_on(i - 1)

        @pl.when(i > nt)
        def done():
            finish(i - 1 - nt)

        return carry

    widen(0)
    lax.fori_loop(0, nt, step, 0)
    widen(1)
    lax.fori_loop(nt, 2 * nt, step, 0)
    finish(nt - 1)

    def drain(t, carry):
        to_core(t).wait_send()
        to_core(nt + t).wait_send()
        to_chip(t).wait_send()
        return carry

    lax.fori_loop(0, nt, drain, 0)
    for phase in range(2):
        for i in range(1, nz):
            gather(i, phase).wait_send()


def fused(nz, activations, gate_up):
    rows, width = activations.shape
    depth, pair, columns = gate_up.shape
    nt = columns // TILE
    weights = gate_up.reshape(depth, pair, columns // HALF, HALF).transpose(0, 2, 1, 3)
    slots = min(RESIDENT, nt) + STREAM
    half = rows // 2
    dma = pltpu.SemaphoreType.DMA
    return pl.pallas_call(
        kernel,
        out_shape=jax.ShapeDtypeStruct((rows // 4, columns), jnp.bfloat16),
        in_specs=[
            pl.BlockSpec(memory_space=pltpu.VMEM),
            pl.BlockSpec(memory_space=pl.ANY),
        ],
        out_specs=pl.BlockSpec(memory_space=pltpu.VMEM),
        scratch_shapes=[
            pltpu.VMEM((nz - 1, rows, width), jnp.bfloat16),
            pltpu.VMEM((2, rows, 2 * depth), jnp.bfloat16),
            pltpu.VMEM((slots, 2, depth, pair, HALF), jnp.bfloat16),
            pltpu.VMEM((2 * nt, half, TILE), jnp.bfloat16),
            pltpu.VMEM((2 * nt, half, TILE), jnp.bfloat16),
            pltpu.VMEM((2, half, TILE), jnp.float32),
            pltpu.VMEM((nt, half, TILE), jnp.bfloat16),
            pltpu.VMEM((nt, half, TILE), jnp.bfloat16),
            dma((slots, 2)),
            dma((nz - 1, 2)),
            dma((nz - 1, 2)),
            dma((2 * nt,)),
            dma((2 * nt,)),
            dma((nt,)),
            dma((nt,)),
        ],
        compiler_params=pltpu.CompilerParams(
            collective_id=0, has_side_effects=True, vmem_limit_bytes=60 * 2**20
        ),
    )(activations, weights)


def plain(activations, gate_up):
    gathered = lax.all_gather(activations, "gy", axis=1, tiled=True)
    partial_value = jnp.einsum("rd,dkf->rkf", gathered, gate_up, preferred_element_type=jnp.float32)
    summed = lax.psum_scatter(
        partial_value.astype(jnp.bfloat16), "gx", scatter_dimension=0, tiled=True
    ).astype(jnp.float32)
    hidden = jax.nn.silu(summed[:, 0]) * summed[:, 1]
    return hidden.astype(jnp.bfloat16)


def solution(mesh):
    nx, nz = mesh.shape["gx"], mesh.shape["gy"]

    def on_device(activations, gate_up):
        width, columns = activations.shape[1], gate_up.shape[2]
        if nx == 4 and nz > 1 and width % HALF == 0 and columns % TILE == 0:
            return fused(nz, activations, gate_up)
        return plain(activations, gate_up)

    placed = (P("groups", ("gx", "gy")), P("gx", None, "gy"))
    return jax.shard_map(
        on_device, mesh=mesh, in_specs=placed, out_specs=P(("groups", "gx"), "gy"), check_vma=False
    )
```

```python
import jax
import jax.numpy as jnp
from jax import lax
from jax.experimental import pallas as pl
from jax.experimental.pallas import tpu as pltpu
from jax.sharding import PartitionSpec as P

MESH = pl.DeviceIdType.MESH
TILE = 512
HALF = 128
PARTS = TILE // HALF
SLOTS = 9
LAG = 4


def kernel(
    a, w, out, a_all, a2, wbuf, s1, r1, keep, near, s2, r2,
    wsem, ag_s, ag_r, s1_s, s1_r, s2_s, s2_r,
):
    nz = a_all.shape[0] + 1
    width = a.shape[1]
    block = a.shape[0] // 4
    depth = nz * width
    nt = s2.shape[0]
    slots = wbuf.shape[0]
    z, gx = lax.axis_index("gy"), lax.axis_index("gx")
    x, c = gx // 2, gx % 2
    core_peer = 2 * x + 1 - c
    chip_peer = 2 * (1 - x) + c

    def w_copies(tile):
        slot = tile % slots
        return [
            pltpu.make_async_copy(w.at[:, PARTS * tile + h], wbuf.at[slot, h], wsem.at[slot, h])
            for h in range(PARTS)
        ]

    def load(tile):
        for copy in w_copies(tile):
            copy.start()

    barrier = pltpu.get_barrier_semaphore()
    for i in range(1, nz):
        pl.semaphore_signal(barrier, inc=1, device_id={"gy": (z + i) % nz}, device_id_type=MESH)
    for peer in (core_peer, chip_peer):
        pl.semaphore_signal(barrier, inc=1, device_id={"gx": peer}, device_id_type=MESH)

    def load_first(t, carry):
        load(t)
        return carry

    lax.fori_loop(0, 1, load_first, 0)
    pl.semaphore_wait(barrier, nz + 1)

    def gather(i, phase):
        side = 1 - x if phase == 0 else x
        rows = pl.ds(pl.multiple_of(side * 2 * block, 2 * block), 2 * block)
        return pltpu.make_async_remote_copy(
            src_ref=a.at[rows],
            dst_ref=a_all.at[i - 1, rows],
            send_sem=ag_s.at[i - 1, phase],
            recv_sem=ag_r.at[i - 1, phase],
            device_id={"gy": (z + i) % nz},
            device_id_type=MESH,
        )

    for phase in range(2):
        for i in range(1, nz):
            gather(i, phase).start()
    lax.fori_loop(1, slots, load_first, 0)

    feature = lax.broadcasted_iota(jnp.int32, (HALF, 4 * HALF), 0)
    place = lax.broadcasted_iota(jnp.int32, (HALF, 4 * HALF), 1)
    spread = (place == 2 * feature + jnp.where(place < 2 * HALF, 0, 2 * HALF + 1)).astype(jnp.bfloat16)

    def widen(phase):
        side = 1 - x if phase == 0 else x
        for i in range(nz):
            source = (z + nz - i) % nz
            if i:
                gather(i, phase).wait_recv()
            for q in range(2):
                core = c if q == 0 else 1 - c
                rows = pl.ds(pl.multiple_of((2 * side + core) * block, block), block)
                for j in range(width // HALF):
                    lanes = pl.ds(j * HALF, HALF)
                    piece = a[rows, lanes] if i == 0 else a_all[i - 1, rows, lanes]
                    both = jnp.dot(piece, spread, preferred_element_type=jnp.float32).astype(jnp.bfloat16)
                    to = pl.ds(pl.multiple_of(source * 2 * width + j * 2 * HALF, 2 * HALF), 2 * HALF)
                    a2[pl.ds((2 * phase + q) * 2 * block, block), to] = both[:, : 2 * HALF]
                    a2[pl.ds((2 * phase + q) * 2 * block + block, block), to] = both[:, 2 * HALF :]

    def to_core(i):
        return pltpu.make_async_remote_copy(
            src_ref=s1.at[i], dst_ref=r1.at[i], send_sem=s1_s.at[i], recv_sem=s1_r.at[i],
            device_id={"gx": core_peer}, device_id_type=MESH,
        )

    def to_chip(t):
        return pltpu.make_async_remote_copy(
            src_ref=s2.at[t], dst_ref=r2.at[t], send_sem=s2_s.at[t], recv_sem=s2_r.at[t],
            device_id={"gx": chip_peer}, device_id_type=MESH,
        )

    def pass_on(t):
        to_core(t).wait_recv()
        total = keep[t % 2] + r1[t].astype(jnp.float32)
        s2[t] = total[: 2 * block].astype(jnp.bfloat16)
        to_chip(t).start()
        near[t] = total[2 * block :]

    def finish(t):
        to_chip(t).wait_recv()
        total = near[t] + r2[t].astype(jnp.float32)
        gate, up = total[:block], total[block:]
        hidden = gate / (1.0 + jnp.exp(-gate)) * up
        out[:, pl.ds(pl.multiple_of(t * TILE, TILE), TILE)] = hidden.astype(jnp.bfloat16)

    def step(t, carry):
        for copy in w_copies(t):
            copy.wait()
        slot = t % slots
        weights = jnp.concatenate(
            [wbuf.at[slot, h].reshape(2 * depth, HALF)[...] for h in range(PARTS)], axis=1
        )
        value = jnp.dot(a2[...], weights, preferred_element_type=jnp.float32)
        for side in range(2):
            own = pl.ds(side * 2 * block, 2 * block)
            at = side * 4 * block
            keep[t % 2, own] = value[at : at + 2 * block]
            s1[t, own] = value[at + 2 * block : at + 4 * block].astype(jnp.bfloat16)
        to_core(t).start()

        @pl.when(t + slots < nt)
        def refill():
            load(t + slots)

        @pl.when(t >= 1)
        def send():
            pass_on(t - 1)

        @pl.when(t >= LAG)
        def done():
            finish(t - LAG)

        return carry

    widen(0)
    widen(1)
    lax.fori_loop(0, nt, step, 0)
    pass_on(nt - 1)

    def rest(t, carry):
        finish(t)
        return carry

    lax.fori_loop(max(nt - LAG, 0), nt, rest, 0)

    def drain(t, carry):
        to_core(t).wait_send()
        to_chip(t).wait_send()
        return carry

    lax.fori_loop(0, nt, drain, 0)
    for phase in range(2):
        for i in range(1, nz):
            gather(i, phase).wait_send()


def fused(nz, activations, gate_up):
    rows, width = activations.shape
    depth, pair, columns = gate_up.shape
    nt = columns // TILE
    weights = gate_up.reshape(depth, pair, columns // HALF, HALF).transpose(0, 2, 1, 3)
    slots = min(SLOTS, nt)
    dma = pltpu.SemaphoreType.DMA
    return pl.pallas_call(
        kernel,
        out_shape=jax.ShapeDtypeStruct((rows // 4, columns), jnp.bfloat16),
        in_specs=[
            pl.BlockSpec(memory_space=pltpu.VMEM),
            pl.BlockSpec(memory_space=pl.ANY),
        ],
        out_specs=pl.BlockSpec(memory_space=pltpu.VMEM),
        scratch_shapes=[
            pltpu.VMEM((nz - 1, rows, width), jnp.bfloat16),
            pltpu.VMEM((2 * rows, 2 * depth), jnp.bfloat16),
            pltpu.VMEM((slots, PARTS, depth, pair, HALF), jnp.bfloat16),
            pltpu.VMEM((nt, rows, TILE), jnp.bfloat16),
            pltpu.VMEM((nt, rows, TILE), jnp.bfloat16),
            pltpu.VMEM((2, rows, TILE), jnp.float32),
            pltpu.VMEM((nt, rows // 2, TILE), jnp.float32),
            pltpu.VMEM((nt, rows // 2, TILE), jnp.bfloat16),
            pltpu.VMEM((nt, rows // 2, TILE), jnp.bfloat16),
            dma((slots, PARTS)),
            dma((nz - 1, 2)),
            dma((nz - 1, 2)),
            dma((nt,)),
            dma((nt,)),
            dma((nt,)),
            dma((nt,)),
        ],
        compiler_params=pltpu.CompilerParams(
            collective_id=0, has_side_effects=True, vmem_limit_bytes=60 * 2**20
        ),
    )(activations, weights)


def plain(activations, gate_up):
    gathered = lax.all_gather(activations, "gy", axis=1, tiled=True)
    partial_value = jnp.einsum("rd,dkf->rkf", gathered, gate_up, preferred_element_type=jnp.float32)
    summed = lax.psum_scatter(
        partial_value.astype(jnp.bfloat16), "gx", scatter_dimension=0, tiled=True
    ).astype(jnp.float32)
    hidden = jax.nn.silu(summed[:, 0]) * summed[:, 1]
    return hidden.astype(jnp.bfloat16)


def solution(mesh):
    nx, nz = mesh.shape["gx"], mesh.shape["gy"]

    def on_device(activations, gate_up):
        width, columns = activations.shape[1], gate_up.shape[2]
        if nx == 4 and nz > 1 and width % HALF == 0 and columns % TILE == 0:
            return fused(nz, activations, gate_up)
        return plain(activations, gate_up)

    placed = (P("groups", ("gx", "gy")), P("gx", None, "gy"))
    return jax.shard_map(
        on_device, mesh=mesh, in_specs=placed, out_specs=P(("groups", "gx"), "gy"), check_vma=False
    )
```
